32 devices in a mesh: groups: 2 (over y), cmp: 4 (over x, core), off: 4 (over z).
Axes of the slice: x: 2, y: 2, z: 4, core: 2. Of those that a mesh axis runs over, the one named last changes fastest.
Arguments:
- shot_traces: bfloat16 [8, 2048, 2048], P(('groups', 'off'), 'cmp'), parts along dimension 0, may hold values from -6 to 6
- trace_owner: int32 [8, 2048, 1], P(('groups', 'off'), 'cmp'), parts along dimension 0, may hold values from 0 to 3; in each aligned block of 512 rows (0 to 511, 512 to 1023, ..., all dimensions but the last counted through in order) at most 256 rows name the same one
- trace_bin: int32 [8, 2048], P(('groups', 'off'), 'cmp'), parts along dimension 0, may hold values from 0 to 127, as said below
- nmo_weight: bfloat16 [4, 16, 512, 128], P('off'), may hold values from -0.25 to 0.25
- band_start: int32 [4, 16], P('off'), may hold values from 0 to 1536, as said below
- mute_start: float32 [4], P('off'), may hold values from 0 to 1024
Outputs:
- stack: float32 [1024, 2048], P(('groups', 'cmp'), 'off'), parts along dimension 0
The draws below stay inside these ranges and needn't reach their ends.
There are 2 independent parts, one for each index of `groups`. The reference program is written for one: setup_inputs(seed, part) draws one part's arguments, and reference() takes and returns one part's arrays. A program takes and returns all parts, laid end to end along the dimension named above; an argument that names none is the same for every part. Nothing has to cross between parts.
Inputs may be any that keep to these rules, and one draw needn't show every extreme that they name: `trace_owner`: among the 512 traces of one device, at most 256 have the same owner. `trace_bin`: some bins receive no trace at all. `band_start`: the band of window j starts at 128 * j plus less than 256, or at 1536 where that is earlier.
All inputs are finite; a program needn't handle non-finite values.
Results may differ from the reference program's by a relative error of at most 0.003.
Values may be sent and summed in bfloat16 or wider, within the bound.
A program may use at most 64 MiB of HBM per device.

```python
import math
import jax
import jax.numpy as jnp
import numpy as np
from jax import lax

NS = 2048
WS = 128
NWIN = 16
SPAN = 512
TR_DEV = 512
BIN_DEV = 128
OFFC = 4
TRC = 2048
BINS = 512
CAP = 256
N_CMP = 4


def draw_band_start(key, part):
    key = jax.random.fold_in(key, 7)
    jitter = jax.random.randint(key, (OFFC, NWIN), 0, 2 * WS)
    window_base = jnp.arange(NWIN, dtype=jnp.int32)[None, :] * WS
    return jnp.minimum(window_base + jitter, NS - SPAN).astype(jnp.int32)


def draw_trace_bin(key, part):
    key = jax.random.fold_in(key, 11)
    order_key, pick_key = jax.random.split(key)
    vacant = BIN_DEV // 8
    inner = (jax.random.permutation(order_key, BIN_DEV - 2) + 1).astype(jnp.int32)
    kept = jnp.concatenate([jnp.zeros((1,), jnp.int32), inner[vacant:], jnp.full((1,), BIN_DEV - 1, jnp.int32)])
    picks = jax.random.randint(pick_key, (OFFC, TRC), 0, BIN_DEV - vacant)
    return kept[picks].astype(jnp.int32)


def strengthened(array, own_key, source, target, parts, factor):
    owner, partner = [(jnp.arange(array.shape[position]) // (array.shape[position] // parts)).reshape([-1 if axis == position else 1 for axis in range(array.ndim)]) for position in (source, target)]
    chosen = jax.random.permutation(own_key, parts)[partner]
    strong = (owner == chosen) | (owner == (partner + parts // 2) % parts)
    return jnp.where(strong, factor * array, array)


def block_scale(stream_key, dims, cuts, smallest, largest):
    def one(position, blocks):
        heights = jax.random.uniform(jax.random.fold_in(jax.random.fold_in(stream_key, 6), position), (blocks,), jnp.float32, smallest / len(cuts), largest / len(cuts))
        return jnp.repeat(jnp.exp(heights), dims[position] // blocks).reshape((-1,) + (1,) * (len(dims) - position - 1))

    loudness = one(*cuts[0])
    for cut in cuts[1:]:
        loudness = loudness * one(*cut)
    return loudness


def assign_block(rng, own, number, rows, count, top, most, lean):
    sequence = jax.random.permutation(rng, count)
    packed, common = load_shares(count, rows * top, most, lean, True), load_shares(count, rows * top, most, lean, False)
    places = jnp.arange(count)

    def named(tallies, rotation):
        used = int((tallies > 0).sum())
        fixed = max(1, used // 4)
        moved = fixed + (places - fixed + rotation * (used - fixed)) % max(1, count - fixed)
        return jnp.zeros((count,), jnp.int32).at[sequence[jnp.where(places < fixed, places, moved)]].set(jnp.asarray(tallies, jnp.int32))

    tallies = jnp.where(number % 4 == 0, named(packed, number // 4), named(common, number - number // 4 - 1))
    mixed = jax.random.permutation(jax.random.fold_in(own, 3), count)
    donor, receiver = mixed[0:count // 2 * 2:2], mixed[1:count // 2 * 2:2]
    room = jnp.minimum(tallies[donor] - 1, most - tallies[receiver]) // 2
    room = jnp.where((donor == sequence[0]) | (receiver == sequence[0]) | (tallies[receiver] == 0), 0, jnp.maximum(room, 0))
    moved = jax.random.randint(jax.random.fold_in(own, 4), (count // 2,), 0, 1 << 20) % (room + 1)
    tallies = tallies.at[donor].add(-moved).at[receiver].add(moved)
    items = jnp.searchsorted(jnp.cumsum(tallies), jnp.arange(rows * top), side="right").astype(jnp.int32)
    table = items.reshape(top, rows).T
    table = table[jax.random.permutation(jax.random.fold_in(own, 1), rows)]
    rotation = jax.random.randint(jax.random.fold_in(own, 2), (rows, 1), 0, top)
    return jnp.take_along_axis(table, (jnp.arange(top)[None, :] + rotation) % top, axis=1)


def load_shares(amount, total, reach, skew, full):
    weights = [(1 << 20) // math.isqrt(grade ** skew) + 1 for grade in range(1, amount + 1)]
    largest = reach if full else min(reach, max(-(-total // amount), total * weights[0] // sum(weights)))
    least = 1 if total - largest >= amount - 1 else 0
    given, spare = [largest] + [least] * (amount - 1), total - largest - least * (amount - 1)
    while spare > 0:
        movable = [i for i in range(1, amount) if given[i] < largest] or [i for i in range(1, amount) if given[i] < reach]
        whole, budget = sum([weights[i] for i in movable]), spare
        for i in movable:
            extra = min(reach - given[i], max(1, budget * weights[i] // whole), spare)
            given[i] = given[i] + extra
            spare = spare - extra
    return np.array(given)


def scatter_about(stream_key, shape, spread, limit, shards=(), kind=jnp.bfloat16):
    level = block_scale(stream_key, shape, shards, -0.22, 0.18) if shards else 1.0
    result = jax.random.normal(stream_key, shape, jnp.float32) * spread * level
    return jnp.minimum(jnp.maximum(result, -limit), limit).astype(kind)


def heavy_noise(key, extent, scale, reach, cuts, heavy, kind=jnp.bfloat16):
    values = scale * jax.random.normal(key, extent, jnp.float32)
    if cuts:
        values = values * block_scale(key, extent, cuts, -0.22, 0.18)
    return jnp.clip(strengthened(values, jax.random.fold_in(key, 3), *heavy), -reach, reach).astype(kind)


def setup_inputs(seed: int = 0, part: int = 0) -> dict:
    key_list = jax.random.split(jax.random.key(seed), 7)
    own_keys = jax.random.split(jax.random.fold_in(key_list[6], part), 7)
    shot_traces = heavy_noise(own_keys[0], (OFFC, TRC, NS), 1.0, 6.0, ((0, 4), (1, 4)), (0, 2, 4, 2.0))
    trace_owner_keys = jax.random.split(jax.random.fold_in(own_keys[1], 1), OFFC * TRC // TR_DEV)
    trace_owner_turns = jax.random.permutation(jax.random.fold_in(own_keys[1], 3), OFFC * TRC // TR_DEV)
    trace_owner = jax.vmap(lambda own, number: assign_block(jax.random.fold_in(own_keys[1], 2), own, number, TR_DEV, N_CMP, 1, CAP, 2))(trace_owner_keys, trace_owner_turns).reshape((OFFC, TRC, 1))
    trace_bin = draw_trace_bin(jax.random.fold_in(jax.random.fold_in(key_list[6], part), 71), part)
    nmo_weight = scatter_about(key_list[3], (OFFC, NWIN, SPAN, WS), SPAN ** -0.5, 0.25, ((0, 4),))
    band_start = draw_band_start(jax.random.fold_in(key_list[6], 71), part)
    mute_start = jnp.clip(1024.0 * jax.random.uniform(key_list[5], (OFFC,), jnp.float32) ** block_scale(key_list[5], (OFFC,), ((0, 4),), -0.2, 0.2), 0.0, 1024.0)
    return {"shot_traces": shot_traces, "trace_owner": trace_owner, "trace_bin": trace_bin, "nmo_weight": nmo_weight, "band_start": band_start, "mute_start": mute_start}


ramp_width = 64.0


def correct_traces(traces, weight, starts, mute_onset):
    pieces = []
    for window in range(weight.shape[0]):
        source = lax.dynamic_slice_in_dim(traces, starts[window], weight.shape[1], 1)
        pieces.append(jnp.dot(source, weight[window], preferred_element_type=jnp.float32))
    shifted = jnp.concatenate(pieces, axis=1)
    sample_time = jnp.arange(shifted.shape[1], dtype=jnp.float32)
    taper_curve = jnp.clip((sample_time - mute_onset) / ramp_width, 0.0, 1.0)
    return (shifted * taper_curve[None, :]).astype(jnp.bfloat16)


def reference(shot_traces, trace_owner, trace_bin, nmo_weight, band_start, mute_start):
    def one_class(carry, inputs):
        totals, counts = carry
        traces, owner_index, local_bin, weight, starts, mute_onset = inputs
        corrected = correct_traces(traces, weight, starts, mute_onset)
        global_bin = (owner_index[:, 0] * BIN_DEV + local_bin).astype(jnp.int32)
        totals = totals + jax.ops.segment_sum(corrected.astype(jnp.float32), global_bin, num_segments=BINS)
        counts = counts + jax.ops.segment_sum(jnp.ones(global_bin.shape, jnp.float32), global_bin, num_segments=BINS)
        return (totals, counts), None

    initial = (jnp.zeros((BINS, NS), jnp.float32), jnp.zeros((BINS,), jnp.float32))
    (totals, counts), unused = lax.scan(one_class, initial, (shot_traces, trace_owner, trace_bin, nmo_weight, band_start, mute_start))
    return totals / jnp.maximum(counts, 1.0)[:, None]
```

```python
import jax
import jax.numpy as jnp
from jax import lax
from jax.experimental import pallas as pl
from jax.experimental.pallas import tpu as pltpu
from jax.sharding import PartitionSpec as P

MESH = pl.DeviceIdType.MESH
BIN_DEV = 128
WIDTH = 256
SPREAD = 384

ramp_width = 64.0


def correct_traces(traces, weight, starts, mute_onset):
    pieces = []
    for window in range(weight.shape[0]):
        source = lax.dynamic_slice_in_dim(traces, starts[window], weight.shape[1], 1)
        pieces.append(jnp.dot(source, weight[window], preferred_element_type=jnp.float32))
    shifted = jnp.concatenate(pieces, axis=1)
    sample_time = jnp.arange(shifted.shape[1], dtype=jnp.float32)
    taper_curve = jnp.clip((sample_time - mute_onset) / ramp_width, 0.0, 1.0)
    return (shifted * taper_curve[None, :]).astype(jnp.bfloat16)


def stack_rows(flat_traces, flat_bins):
    selector = jnp.arange(BIN_DEV, dtype=jnp.int32)[:, None] == flat_bins[None, :]
    partial_stack = jnp.dot(
        selector.astype(jnp.bfloat16), flat_traces, preferred_element_type=jnp.float32
    )
    local_fold = jnp.sum(selector.astype(jnp.float32), axis=1)
    return (partial_stack, local_fold)


def on_device(shot_traces, trace_owner, trace_bin, nmo_weight, band_start, mute_start):
    peer_count = lax.axis_size("cmp")
    traces = shot_traces[0]
    owner_index = trace_owner[0, :, 0]
    local_bin = trace_bin[0]
    weight = nmo_weight[0]
    starts = band_start[0]
    mute_onset = mute_start[0]
    trace_count = traces.shape[0]
    samples = traces.shape[1]
    capacity = 2 * trace_count // peer_count
    member = (owner_index[:, None] == jnp.arange(peer_count, dtype=jnp.int32)[None, :]).astype(
        jnp.int32
    )
    earlier = jnp.cumsum(member, axis=0) - member
    slot_index = jnp.sum(earlier * member, axis=1)
    target = owner_index * capacity + slot_index
    bin_buffer = jnp.full((peer_count * capacity,), -1, jnp.int32).at[target].set(local_bin)
    bin_buffer = bin_buffer.reshape(peer_count, capacity)
    buffer = jnp.zeros((peer_count * capacity, samples), jnp.bfloat16).at[target].set(traces)
    slots = lax.all_to_all(
        buffer.reshape(peer_count, capacity, samples),
        "cmp",
        split_axis=0,
        concat_axis=0,
        tiled=True,
    )
    slot_bins = lax.all_to_all(bin_buffer, "cmp", split_axis=0, concat_axis=0, tiled=True)
    flat_slots = slots.reshape(-1, samples)
    repaired = correct_traces(flat_slots, weight, starts, mute_onset)
    arrived = repaired.reshape(slots.shape)
    partial_stack, local_fold = stack_rows(arrived.reshape(-1, samples), slot_bins.reshape(-1))
    fold_count = lax.psum(local_fold, "off")
    stack_share = lax.psum_scatter(partial_stack, "off", scatter_dimension=1, tiled=True)
    return stack_share / jnp.maximum(fold_count, 1.0)[:, None]


def fused(
    traces_hbm, weight_hbm, owner_ref, bin_ref, starts_ref, mute_ref,
    out_ref, fold_ref,
    traces, weight, padded, shifted_weight, selector,
    keep_core, send_core, recv_core,
    keep_x, send_x, recv_x, send_z, recv_z,
    fold_core_out, fold_core_in, fold_x_out, fold_x_in, fold_z_in,
    load_sem, weight_sem,
    core_send_sem, core_recv_sem, x_send_sem, x_recv_sem, z_send_sem, z_recv_sem,
    fold_send_sem, fold_recv_sem,
):
    rows, samples = traces.shape
    span = weight.shape[2]
    chunks = weight.shape[0]
    c = lax.axis_index("cmp")
    z = lax.axis_index("off")
    nz = 4
    core_peer = c + 1 - 2 * lax.rem(c, 2)
    x_peer = lax.rem(c + 2, 4)
    band = span + SPREAD

    barrier = pltpu.get_barrier_semaphore()
    pl.semaphore_signal(barrier, inc=1, device_id={"cmp": core_peer}, device_id_type=MESH)
    pl.semaphore_signal(barrier, inc=1, device_id={"cmp": x_peer}, device_id_type=MESH)
    for step in range(1, nz):
        pl.semaphore_signal(
            barrier, inc=1, device_id={"off": lax.rem(z + step, nz)}, device_id_type=MESH
        )

    def pair_of(m):
        return 2 * lax.rem(z + 1 + m // 2, nz) + m % 2

    load = pltpu.make_async_copy(traces_hbm, traces, load_sem)
    load.start()

    def weight_load(m):
        return pltpu.make_async_copy(
            weight_hbm.at[pl.ds(2 * pair_of(m), 2)], weight.at[m], weight_sem.at[m]
        )

    def begin(m, carry):
        weight_load(m).start()
        return carry

    lax.fori_loop(0, chunks, begin, 0)

    owner = owner_ref[...]
    other_core = jnp.where(lax.rem(owner, 2) == lax.rem(c, 2), 0, 1)
    other_x = jnp.where(owner // 2 == c // 2, 0, 1)
    place = (2 * other_core + other_x) * BIN_DEV + bin_ref[...]
    line = lax.broadcasted_iota(jnp.int32, (4 * BIN_DEV, rows), 0)
    selector[...] = jnp.where(line == place, 1.0, 0.0).astype(jnp.bfloat16)
    fold = lax.dot_general(
        jnp.ones((8, rows), jnp.bfloat16),
        selector[...],
        (((1,), (1,)), ((), ())),
        preferred_element_type=jnp.float32,
    )
    fold_core_out[...] = fold[:, 2 * BIN_DEV :]
    padded[:, 0:SPREAD] = jnp.zeros((2, SPREAD, 128), jnp.float32)
    padded[:, SPREAD + span :] = jnp.zeros((2, SPREAD, 128), jnp.float32)
    load.wait()

    def core_copy(m):
        return pltpu.make_async_remote_copy(
            src_ref=send_core.at[m], dst_ref=recv_core.at[m],
            send_sem=core_send_sem.at[m], recv_sem=core_recv_sem.at[m],
            device_id={"cmp": core_peer}, device_id_type=MESH,
        )

    def x_copy(m):
        return pltpu.make_async_remote_copy(
            src_ref=send_x.at[m], dst_ref=recv_x.at[m],
            send_sem=x_send_sem.at[m], recv_sem=x_recv_sem.at[m],
            device_id={"cmp": x_peer}, device_id_type=MESH,
        )

    def z_copy(m):
        return pltpu.make_async_remote_copy(
            src_ref=send_z.at[m], dst_ref=recv_z.at[m],
            send_sem=z_send_sem.at[m], recv_sem=z_recv_sem.at[m],
            device_id={"off": lax.rem(z + 1 + m // 2, nz)}, device_id_type=MESH,
        )

    def fold_copy(source, target, slot, device):
        return pltpu.make_async_remote_copy(
            src_ref=source, dst_ref=target,
            send_sem=fold_send_sem.at[slot], recv_sem=fold_recv_sem.at[slot],
            device_id=device, device_id_type=MESH,
        )

    def correct(m):
        weight_load(m).wait()
        first = pair_of(m) * WIDTH
        base = jnp.minimum(first, samples - band)
        for half in range(2):
            start = starts_ref[2 * pair_of(m) + half]
            lead = jnp.clip(start - base, 0, SPREAD)
            padded[half, SPREAD : SPREAD + span] = weight[m, half].astype(jnp.float32)
            shifted_weight[:, half * 128 : half * 128 + 128] = padded[
                half, pl.ds(SPREAD - lead, band)
            ].astype(jnp.bfloat16)
        source = traces[:, pl.ds(pl.multiple_of(base, 128), band)]
        shifted = jnp.dot(source, shifted_weight[...], preferred_element_type=jnp.float32)
        time = first + lax.broadcasted_iota(jnp.int32, (1, WIDTH), 1)
        taper = jnp.clip((time.astype(jnp.float32) - mute_ref[0]) / ramp_width, 0.0, 1.0)
        corrected = (shifted * taper).astype(jnp.bfloat16)
        partial = jnp.dot(selector[...], corrected, preferred_element_type=jnp.float32)
        keep_core[m] = partial[: 2 * BIN_DEV]
        send_core[m] = partial[2 * BIN_DEV :].astype(jnp.bfloat16)

    def end_core(m):
        core_copy(m).wait_recv()
        total = keep_core[m] + recv_core[m].astype(jnp.float32)
        keep_x[m] = total[:BIN_DEV]
        send_x[m] = total[BIN_DEV:].astype(jnp.bfloat16)
        x_copy(m).start()

    def x_total(m):
        x_copy(m).wait_recv()
        return keep_x[m] + recv_x[m].astype(jnp.float32)

    def end_x(m):
        send_z[m] = x_total(m).astype(jnp.bfloat16)
        z_copy(m).start()

    correct(0)
    pl.semaphore_wait(barrier, nz + 1)
    core_copy(0).start()
    fold_core = fold_copy(fold_core_out, fold_core_in, 0, {"cmp": core_peer})
    fold_core.start()

    def step(m, carry):
        correct(m)
        core_copy(m).start()
        end_core(m - 1)

        @pl.when(m >= 3)
        def _():
            end_x(m - 3)

        return carry

    lax.fori_loop(1, chunks, step, 0)
    end_core(chunks - 1)

    fold_core.wait_recv()
    fold = fold[:, : 2 * BIN_DEV] + fold_core_in[...]
    fold_x_out[0] = fold[:, BIN_DEV:]
    fold_x = fold_copy(fold_x_out.at[0], fold_x_in, 1, {"cmp": x_peer})
    fold_x.start()
    for m in range(chunks - 3, chunks - 2):
        end_x(m)
    fold_x.wait_recv()
    fold = fold[:, :BIN_DEV] + fold_x_in[...]
    fold_x_out[1] = fold
    fold_z = []
    for away in range(1, nz):
        copy = fold_copy(
            fold_x_out.at[1], fold_z_in.at[away - 1], 1 + away, {"off": lax.rem(z + away, nz)}
        )
        copy.start()
        fold_z.append(copy)

    for half in range(2):
        out_ref[:, half * WIDTH : half * WIDTH + WIDTH] = x_total(chunks - 2 + half)
    for copy in fold_z:
        copy.wait_recv()
    for away in range(1, nz):
        fold = fold + fold_z_in[away - 1]
    fold_ref[...] = fold
    for m in range(chunks - 2):
        z_copy(m).wait_recv()
        half = m % 2
        out_ref[:, half * WIDTH : half * WIDTH + WIDTH] += recv_z[m].astype(jnp.float32)

    def drain(m, carry):
        core_copy(m).wait_send()
        x_copy(m).wait_send()
        return carry

    lax.fori_loop(0, chunks, drain, 0)

    def drain_z(m, carry):
        z_copy(m).wait_send()
        return carry

    lax.fori_loop(0, chunks - 2, drain_z, 0)
    fold_core.wait_send()
    fold_x.wait_send()
    for copy in fold_z:
        copy.wait_send()


def on_device_fused(shot_traces, trace_owner, trace_bin, nmo_weight, band_start, mute_start):
    rows, samples = shot_traces.shape[1:]
    windows, span, ws = nmo_weight.shape[1:]
    chunks = samples // WIDTH
    f32, bf16 = jnp.float32, jnp.bfloat16
    any_space = pl.BlockSpec(memory_space=pl.ANY)
    vmem = pl.BlockSpec(memory_space=pltpu.VMEM)
    smem = pl.BlockSpec(memory_space=pltpu.SMEM)
    dma = pltpu.SemaphoreType.DMA
    totals, fold = pl.pallas_call(
        fused,
        out_shape=(
            jax.ShapeDtypeStruct((BIN_DEV, samples // 4), f32),
            jax.ShapeDtypeStruct((8, BIN_DEV), f32),
        ),
        in_specs=[any_space, any_space, vmem, vmem, smem, smem],
        out_specs=(vmem, vmem),
        scratch_shapes=[
            pltpu.VMEM((rows, samples), bf16),
            pltpu.VMEM((chunks, 2, span, ws), bf16),
            pltpu.VMEM((2, span + 2 * SPREAD, ws), f32),
            pltpu.VMEM((span + SPREAD, WIDTH), bf16),
            pltpu.VMEM((4 * BIN_DEV, rows), bf16),
            pltpu.VMEM((chunks, 2 * BIN_DEV, WIDTH), f32),
            pltpu.VMEM((chunks, 2 * BIN_DEV, WIDTH), bf16),
            pltpu.VMEM((chunks, 2 * BIN_DEV, WIDTH), bf16),
            pltpu.VMEM((chunks, BIN_DEV, WIDTH), f32),
            pltpu.VMEM((chunks, BIN_DEV, WIDTH), bf16),
            pltpu.VMEM((chunks, BIN_DEV, WIDTH), bf16),
            pltpu.VMEM((chunks - 2, BIN_DEV, WIDTH), bf16),
            pltpu.VMEM((chunks - 2, BIN_DEV, WIDTH), bf16),
            pltpu.VMEM((8, 2 * BIN_DEV), f32),
            pltpu.VMEM((8, 2 * BIN_DEV), f32),
            pltpu.VMEM((2, 8, BIN_DEV), f32),
            pltpu.VMEM((8, BIN_DEV), f32),
            pltpu.VMEM((3, 8, BIN_DEV), f32),
            dma,
            dma((chunks,)),
            dma((chunks,)),
            dma((chunks,)),
            dma((chunks,)),
            dma((chunks,)),
            dma((chunks - 2,)),
            dma((chunks - 2,)),
            dma((5,)),
            dma((5,)),
        ],
        compiler_params=pltpu.CompilerParams(
            collective_id=0, has_side_effects=True, vmem_limit_bytes=48 * 2**20
        ),
        cost_estimate=pl.CostEstimate(
            flops=4 * rows * samples * span, bytes_accessed=4 * rows * samples, transcendentals=0
        ),
    )(
        shot_traces[0],
        nmo_weight[0],
        trace_owner.reshape(1, rows),
        trace_bin,
        band_start[0],
        mute_start,
    )
    return totals / jnp.maximum(fold[0], 1.0)[:, None]


def solution(mesh):
    direct = mesh.shape["cmp"] == 4 and mesh.shape["off"] == 4
    return jax.shard_map(
        on_device_fused if direct else on_device,
        mesh=mesh,
        in_specs=(
            P(("groups", "off"), "cmp", None),
            P(("groups", "off"), "cmp", None),
            P(("groups", "off"), "cmp"),
            P("off", None, None, None),
            P("off", None),
            P("off"),
        ),
        out_specs=P(("groups", "cmp"), "off"),
        check_vma=False,
    )
```

```python
import jax
import jax.numpy as jnp
from jax import lax
from jax.experimental import pallas as pl
from jax.experimental.pallas import tpu as pltpu
from jax.sharding import PartitionSpec as P

MESH = pl.DeviceIdType.MESH
BIN_DEV = 128
WIDTH = 256
SPREAD = 384

ramp_width = 64.0


def correct_traces(traces, weight, starts, mute_onset):
    pieces = []
    for window in range(weight.shape[0]):
        source = lax.dynamic_slice_in_dim(traces, starts[window], weight.shape[1], 1)
        pieces.append(jnp.dot(source, weight[window], preferred_element_type=jnp.float32))
    shifted = jnp.concatenate(pieces, axis=1)
    sample_time = jnp.arange(shifted.shape[1], dtype=jnp.float32)
    taper_curve = jnp.clip((sample_time - mute_onset) / ramp_width, 0.0, 1.0)
    return (shifted * taper_curve[None, :]).astype(jnp.bfloat16)


def stack_rows(flat_traces, flat_bins):
    selector = jnp.arange(BIN_DEV, dtype=jnp.int32)[:, None] == flat_bins[None, :]
    partial_stack = jnp.dot(
        selector.astype(jnp.bfloat16), flat_traces, preferred_element_type=jnp.float32
    )
    local_fold = jnp.sum(selector.astype(jnp.float32), axis=1)
    return (partial_stack, local_fold)


def on_device(shot_traces, trace_owner, trace_bin, nmo_weight, band_start, mute_start):
    peer_count = lax.axis_size("cmp")
    traces = shot_traces[0]
    owner_index = trace_owner[0, :, 0]
    local_bin = trace_bin[0]
    weight = nmo_weight[0]
    starts = band_start[0]
    mute_onset = mute_start[0]
    trace_count = traces.shape[0]
    samples = traces.shape[1]
    capacity = 2 * trace_count // peer_count
    member = (owner_index[:, None] == jnp.arange(peer_count, dtype=jnp.int32)[None, :]).astype(
        jnp.int32
    )
    earlier = jnp.cumsum(member, axis=0) - member
    slot_index = jnp.sum(earlier * member, axis=1)
    target = owner_index * capacity + slot_index
    bin_buffer = jnp.full((peer_count * capacity,), -1, jnp.int32).at[target].set(local_bin)
    bin_buffer = bin_buffer.reshape(peer_count, capacity)
    buffer = jnp.zeros((peer_count * capacity, samples), jnp.bfloat16).at[target].set(traces)
    slots = lax.all_to_all(
        buffer.reshape(peer_count, capacity, samples),
        "cmp",
        split_axis=0,
        concat_axis=0,
        tiled=True,
    )
    slot_bins = lax.all_to_all(bin_buffer, "cmp", split_axis=0, concat_axis=0, tiled=True)
    flat_slots = slots.reshape(-1, samples)
    repaired = correct_traces(flat_slots, weight, starts, mute_onset)
    arrived = repaired.reshape(slots.shape)
    partial_stack, local_fold = stack_rows(arrived.reshape(-1, samples), slot_bins.reshape(-1))
    fold_count = lax.psum(local_fold, "off")
    stack_share = lax.psum_scatter(partial_stack, "off", scatter_dimension=1, tiled=True)
    return stack_share / jnp.maximum(fold_count, 1.0)[:, None]


def fused(
    traces_hbm, weight_hbm, owner_hbm, bin_hbm, starts_hbm, mute_hbm,
    out_ref, fold_ref,
    owner_ref, bin_ref, starts_ref, mute_ref,
    traces, weight, padded, shifted_weight, selector,
    keep_core, send_core, recv_core,
    keep_x, send_x, recv_x, send_z, recv_z,
    fold_core_out, fold_core_in, fold_x_out, fold_x_in, fold_z_in,
    load_sem, small_sem, weight_sem,
    core_send_sem, core_recv_sem, x_send_sem, x_recv_sem, z_send_sem, z_recv_sem,
    fold_send_sem, fold_recv_sem,
):
    rows, samples = traces.shape
    span = weight.shape[2]
    chunks = weight.shape[0]
    c = lax.axis_index("cmp")
    z = lax.axis_index("off")
    nz = 4
    core_peer = c + 1 - 2 * lax.rem(c, 2)
    x_peer = lax.rem(c + 2, 4)
    band = span + SPREAD

    barrier = pltpu.get_barrier_semaphore()
    pl.semaphore_signal(barrier, inc=1, device_id={"cmp": core_peer}, device_id_type=MESH)
    pl.semaphore_signal(barrier, inc=1, device_id={"cmp": x_peer}, device_id_type=MESH)
    for step in range(1, nz):
        pl.semaphore_signal(
            barrier, inc=1, device_id={"off": lax.rem(z + step, nz)}, device_id_type=MESH
        )

    def pair_of(m):
        return 2 * lax.rem(z + 1 + m // 2, nz) + m % 2

    small = [
        pltpu.make_async_copy(source, target, small_sem.at[slot])
        for slot, (source, target) in enumerate(
            (
                (owner_hbm, owner_ref),
                (bin_hbm, bin_ref),
                (starts_hbm, starts_ref),
                (mute_hbm, mute_ref),
            )
        )
    ]
    for copy in small:
        copy.start()
    load = pltpu.make_async_copy(traces_hbm, traces, load_sem)
    load.start()

    def weight_load(m):
        return pltpu.make_async_copy(
            weight_hbm.at[pl.ds(2 * pair_of(m), 2)], weight.at[m], weight_sem.at[m]
        )

    def begin(m, carry):
        weight_load(m).start()
        return carry

    lax.fori_loop(0, chunks, begin, 0)

    for copy in small:
        copy.wait()
    owner = owner_ref[...]
    other_core = jnp.where(lax.rem(owner, 2) == lax.rem(c, 2), 0, 1)
    other_x = jnp.where(owner // 2 == c // 2, 0, 1)
    place = (2 * other_core + other_x) * BIN_DEV + bin_ref[...]
    line = lax.broadcasted_iota(jnp.int32, (4 * BIN_DEV, rows), 0)
    selector[...] = jnp.where(line == place, 1.0, 0.0).astype(jnp.bfloat16)
    fold = lax.dot_general(
        jnp.ones((8, rows), jnp.bfloat16),
        selector[...],
        (((1,), (1,)), ((), ())),
        preferred_element_type=jnp.float32,
    )
    fold_core_out[...] = fold[:, 2 * BIN_DEV :]
    padded[:, 0:SPREAD] = jnp.zeros((2, SPREAD, 128), jnp.float32)
    padded[:, SPREAD + span :] = jnp.zeros((2, SPREAD, 128), jnp.float32)
    load.wait()

    def core_copy(m):
        return pltpu.make_async_remote_copy(
            src_ref=send_core.at[m], dst_ref=recv_core.at[m],
            send_sem=core_send_sem.at[m], recv_sem=core_recv_sem.at[m],
            device_id={"cmp": core_peer}, device_id_type=MESH,
        )

    def x_copy(m):
        return pltpu.make_async_remote_copy(
            src_ref=send_x.at[m], dst_ref=recv_x.at[m],
            send_sem=x_send_sem.at[m], recv_sem=x_recv_sem.at[m],
            device_id={"cmp": x_peer}, device_id_type=MESH,
        )

    def z_copy(m):
        return pltpu.make_async_remote_copy(
            src_ref=send_z.at[m], dst_ref=recv_z.at[m],
            send_sem=z_send_sem.at[m], recv_sem=z_recv_sem.at[m],
            device_id={"off": lax.rem(z + 1 + m // 2, nz)}, device_id_type=MESH,
        )

    def fold_copy(source, target, slot, device):
        return pltpu.make_async_remote_copy(
            src_ref=source, dst_ref=target,
            send_sem=fold_send_sem.at[slot], recv_sem=fold_recv_sem.at[slot],
            device_id=device, device_id_type=MESH,
        )

    def correct(m):
        weight_load(m).wait()
        first = pair_of(m) * WIDTH
        base = jnp.minimum(first, samples - band)
        for half in range(2):
            start = starts_ref[2 * pair_of(m) + half]
            lead = jnp.clip(start - base, 0, SPREAD)
            padded[half, SPREAD : SPREAD + span] = weight[m, half].astype(jnp.float32)
            shifted_weight[:, half * 128 : half * 128 + 128] = padded[
                half, pl.ds(SPREAD - lead, band)
            ].astype(jnp.bfloat16)
        source = traces[:, pl.ds(pl.multiple_of(base, 128), band)]
        shifted = jnp.dot(source, shifted_weight[...], preferred_element_type=jnp.float32)
        time = first + lax.broadcasted_iota(jnp.int32, (1, WIDTH), 1)
        taper = jnp.clip((time.astype(jnp.float32) - mute_ref[0]) / ramp_width, 0.0, 1.0)
        corrected = (shifted * taper).astype(jnp.bfloat16)
        partial = jnp.dot(selector[...], corrected, preferred_element_type=jnp.float32)
        keep_core[m] = partial[: 2 * BIN_DEV]
        send_core[m] = partial[2 * BIN_DEV :].astype(jnp.bfloat16)

    def end_core(m):
        core_copy(m).wait_recv()
        total = keep_core[m] + recv_core[m].astype(jnp.float32)
        keep_x[m] = total[:BIN_DEV]
        send_x[m] = total[BIN_DEV:].astype(jnp.bfloat16)
        x_copy(m).start()

    def x_total(m):
        x_copy(m).wait_recv()
        return keep_x[m] + recv_x[m].astype(jnp.float32)

    def end_x(m):
        send_z[m] = x_total(m).astype(jnp.bfloat16)
        z_copy(m).start()

    correct(0)
    pl.semaphore_wait(barrier, nz + 1)
    core_copy(0).start()
    fold_core = fold_copy(fold_core_out, fold_core_in, 0, {"cmp": core_peer})
    fold_core.start()

    def step(m, carry):
        correct(m)
        core_copy(m).start()
        end_core(m - 1)

        @pl.when(m >= 3)
        def _():
            end_x(m - 3)

        return carry

    lax.fori_loop(1, chunks, step, 0)
    end_core(chunks - 1)

    fold_core.wait_recv()
    fold = fold[:, : 2 * BIN_DEV] + fold_core_in[...]
    fold_x_out[0] = fold[:, BIN_DEV:]
    fold_x = fold_copy(fold_x_out.at[0], fold_x_in, 1, {"cmp": x_peer})
    fold_x.start()
    for m in range(chunks - 3, chunks - 2):
        end_x(m)
    fold_x.wait_recv()
    fold = fold[:, :BIN_DEV] + fold_x_in[...]
    fold_x_out[1] = fold
    fold_z = []
    for away in range(1, nz):
        copy = fold_copy(
            fold_x_out.at[1], fold_z_in.at[away - 1], 1 + away, {"off": lax.rem(z + away, nz)}
        )
        copy.start()
        fold_z.append(copy)

    for half in range(2):
        out_ref[:, half * WIDTH : half * WIDTH + WIDTH] = x_total(chunks - 2 + half)
    for copy in fold_z:
        copy.wait_recv()
    for away in range(1, nz):
        fold = fold + fold_z_in[away - 1]
    fold_ref[...] = fold
    for m in range(chunks - 2):
        z_copy(m).wait_recv()
        half = m % 2
        out_ref[:, half * WIDTH : half * WIDTH + WIDTH] += recv_z[m].astype(jnp.float32)

    def drain(m, carry):
        core_copy(m).wait_send()
        x_copy(m).wait_send()
        return carry

    lax.fori_loop(0, chunks, drain, 0)

    def drain_z(m, carry):
        z_copy(m).wait_send()
        return carry

    lax.fori_loop(0, chunks - 2, drain_z, 0)
    fold_core.wait_send()
    fold_x.wait_send()
    for copy in fold_z:
        copy.wait_send()


def on_device_fused(shot_traces, trace_owner, trace_bin, nmo_weight, band_start, mute_start):
    rows, samples = shot_traces.shape[1:]
    windows, span, ws = nmo_weight.shape[1:]
    chunks = samples // WIDTH
    f32, bf16 = jnp.float32, jnp.bfloat16
    hbm = pl.BlockSpec(memory_space=pltpu.HBM)
    vmem = pl.BlockSpec(memory_space=pltpu.VMEM)
    dma = pltpu.SemaphoreType.DMA
    totals, fold = pl.pallas_call(
        fused,
        out_shape=(
            jax.ShapeDtypeStruct((BIN_DEV, samples // 4), f32),
            jax.ShapeDtypeStruct((8, BIN_DEV), f32),
        ),
        in_specs=[hbm] * 6,
        out_specs=(vmem, vmem),
        scratch_shapes=[
            pltpu.VMEM((1, rows), jnp.int32),
            pltpu.VMEM((1, rows), jnp.int32),
            pltpu.SMEM((windows,), jnp.int32),
            pltpu.SMEM((1,), f32),
            pltpu.VMEM((rows, samples), bf16),
            pltpu.VMEM((chunks, 2, span, ws), bf16),
            pltpu.VMEM((2, span + 2 * SPREAD, ws), f32),
            pltpu.VMEM((span + SPREAD, WIDTH), bf16),
            pltpu.VMEM((4 * BIN_DEV, rows), bf16),
            pltpu.VMEM((chunks, 2 * BIN_DEV, WIDTH), f32),
            pltpu.VMEM((chunks, 2 * BIN_DEV, WIDTH), bf16),
            pltpu.VMEM((chunks, 2 * BIN_DEV, WIDTH), bf16),
            pltpu.VMEM((chunks, BIN_DEV, WIDTH), f32),
            pltpu.VMEM((chunks, BIN_DEV, WIDTH), bf16),
            pltpu.VMEM((chunks, BIN_DEV, WIDTH), bf16),
            pltpu.VMEM((chunks - 2, BIN_DEV, WIDTH), bf16),
            pltpu.VMEM((chunks - 2, BIN_DEV, WIDTH), bf16),
            pltpu.VMEM((8, 2 * BIN_DEV), f32),
            pltpu.VMEM((8, 2 * BIN_DEV), f32),
            pltpu.VMEM((2, 8, BIN_DEV), f32),
            pltpu.VMEM((8, BIN_DEV), f32),
            pltpu.VMEM((3, 8, BIN_DEV), f32),
            dma,
            dma((4,)),
            dma((chunks,)),
            dma((chunks,)),
            dma((chunks,)),
            dma((chunks,)),
            dma((chunks,)),
            dma((chunks - 2,)),
            dma((chunks - 2,)),
            dma((5,)),
            dma((5,)),
        ],
        compiler_params=pltpu.CompilerParams(
            collective_id=0, has_side_effects=True, vmem_limit_bytes=62 * 2**20
        ),
        cost_estimate=pl.CostEstimate(
            flops=4 * rows * samples * span, bytes_accessed=4 * rows * samples, transcendentals=0
        ),
    )(
        shot_traces[0],
        nmo_weight[0],
        trace_owner.reshape(1, rows),
        trace_bin,
        band_start[0],
        mute_start,
    )
    return totals / jnp.maximum(fold[0], 1.0)[:, None]


def solution(mesh):
    direct = mesh.shape["cmp"] == 4 and mesh.shape["off"] == 4
    return jax.shard_map(
        on_device_fused if direct else on_device,
        mesh=mesh,
        in_specs=(
            P(("groups", "off"), "cmp", None),
            P(("groups", "off"), "cmp", None),
            P(("groups", "off"), "cmp"),
            P("off", None, None, None),
            P("off", None),
            P("off"),
        ),
        out_specs=P(("groups", "cmp"), "off"),
        check_vma=False,
    )
```

```python
import jax
import jax.numpy as jnp
from jax import lax
from jax.experimental import pallas as pl
from jax.experimental.pallas import tpu as pltpu
from jax.sharding import PartitionSpec as P

MESH = pl.DeviceIdType.MESH
BIN_DEV = 128
WIDTH = 256
SPREAD = 384

ramp_width = 64.0


def correct_traces(traces, weight, starts, mute_onset):
    pieces = []
    for window in range(weight.shape[0]):
        source = lax.dynamic_slice_in_dim(traces, starts[window], weight.shape[1], 1)
        pieces.append(jnp.dot(source, weight[window], preferred_element_type=jnp.float32))
    shifted = jnp.concatenate(pieces, axis=1)
    sample_time = jnp.arange(shifted.shape[1], dtype=jnp.float32)
    taper_curve = jnp.clip((sample_time - mute_onset) / ramp_width, 0.0, 1.0)
    return (shifted * taper_curve[None, :]).astype(jnp.bfloat16)


def stack_rows(flat_traces, flat_bins):
    selector = jnp.arange(BIN_DEV, dtype=jnp.int32)[:, None] == flat_bins[None, :]
    partial_stack = jnp.dot(
        selector.astype(jnp.bfloat16), flat_traces, preferred_element_type=jnp.float32
    )
    local_fold = jnp.sum(selector.astype(jnp.float32), axis=1)
    return (partial_stack, local_fold)


def on_device(shot_traces, trace_owner, trace_bin, nmo_weight, band_start, mute_start):
    peer_count = lax.axis_size("cmp")
    traces = shot_traces[0]
    owner_index = trace_owner[0, :, 0]
    local_bin = trace_bin[0]
    weight = nmo_weight[0]
    starts = band_start[0]
    mute_onset = mute_start[0]
    trace_count = traces.shape[0]
    samples = traces.shape[1]
    capacity = 2 * trace_count // peer_count
    member = (owner_index[:, None] == jnp.arange(peer_count, dtype=jnp.int32)[None, :]).astype(
        jnp.int32
    )
    earlier = jnp.cumsum(member, axis=0) - member
    slot_index = jnp.sum(earlier * member, axis=1)
    target = owner_index * capacity + slot_index
    bin_buffer = jnp.full((peer_count * capacity,), -1, jnp.int32).at[target].set(local_bin)
    bin_buffer = bin_buffer.reshape(peer_count, capacity)
    buffer = jnp.zeros((peer_count * capacity, samples), jnp.bfloat16).at[target].set(traces)
    slots = lax.all_to_all(
        buffer.reshape(peer_count, capacity, samples),
        "cmp",
        split_axis=0,
        concat_axis=0,
        tiled=True,
    )
    slot_bins = lax.all_to_all(bin_buffer, "cmp", split_axis=0, concat_axis=0, tiled=True)
    flat_slots = slots.reshape(-1, samples)
    repaired = correct_traces(flat_slots, weight, starts, mute_onset)
    arrived = repaired.reshape(slots.shape)
    partial_stack, local_fold = stack_rows(arrived.reshape(-1, samples), slot_bins.reshape(-1))
    fold_count = lax.psum(local_fold, "off")
    stack_share = lax.psum_scatter(partial_stack, "off", scatter_dimension=1, tiled=True)
    return stack_share / jnp.maximum(fold_count, 1.0)[:, None]


def fused(
    traces_hbm, weight_hbm, owner_hbm, bin_hbm, starts_hbm, mute_hbm,
    out_ref, fold_ref,
    owner_ref, bin_ref, starts_ref, mute_ref,
    traces, first_band, weight, padded, shifted_weight, selector,
    keep_core, send_core, recv_core,
    keep_x, send_x, recv_x, send_z, recv_z,
    fold_core_out, fold_core_in, fold_x_out, fold_x_in, fold_z_in,
    load_sem, first_sem, small_sem, weight_sem,
    core_send_sem, core_recv_sem, x_send_sem, x_recv_sem, z_send_sem, z_recv_sem,
    fold_send_sem, fold_recv_sem,
):
    rows, samples = traces.shape
    span = weight.shape[2]
    chunks = weight.shape[0]
    c = lax.axis_index("cmp")
    z = lax.axis_index("off")
    nz = 4
    core_peer = c + 1 - 2 * lax.rem(c, 2)
    x_peer = lax.rem(c + 2, 4)
    band = span + SPREAD

    barrier = pltpu.get_barrier_semaphore()
    pl.semaphore_signal(barrier, inc=1, device_id={"cmp": core_peer}, device_id_type=MESH)
    pl.semaphore_signal(barrier, inc=1, device_id={"cmp": x_peer}, device_id_type=MESH)
    for step in range(1, nz):
        pl.semaphore_signal(
            barrier, inc=1, device_id={"off": lax.rem(z + step, nz)}, device_id_type=MESH
        )

    def pair_of(m):
        return 2 * lax.rem(z + nz - 1 - m // 2, nz) + m % 2

    small = [
        pltpu.make_async_copy(source, target, small_sem.at[slot])
        for slot, (source, target) in enumerate(
            (
                (owner_hbm, owner_ref),
                (bin_hbm, bin_ref),
                (starts_hbm, starts_ref),
                (mute_hbm, mute_ref),
            )
        )
    ]
    for copy in small:
        copy.start()
    def base_of(m):
        pair = pair_of(m)
        last = samples - band
        return WIDTH * pair - (pair // -(-last // WIDTH)) * (WIDTH * pair - last)

    first_load = pltpu.make_async_copy(
        traces_hbm.at[:, pl.ds(pl.multiple_of(base_of(0), 128), band)], first_band, first_sem
    )
    first_load.start()
    load = pltpu.make_async_copy(traces_hbm, traces, load_sem)

    def weight_load(m):
        return pltpu.make_async_copy(
            weight_hbm.at[pl.ds(2 * pair_of(m), 2)], weight.at[m], weight_sem.at[m]
        )

    def begin(m, carry):
        weight_load(m).start()
        return carry

    weight_load(0).start()

    for copy in small:
        copy.wait()
    owner = owner_ref[...]
    other_core = jnp.where(lax.rem(owner, 2) == lax.rem(c, 2), 0, 1)
    other_x = jnp.where(owner // 2 == c // 2, 0, 1)
    place = (2 * other_core + other_x) * BIN_DEV + bin_ref[...]
    line = lax.broadcasted_iota(jnp.int32, (4 * BIN_DEV, rows), 0)
    selector[...] = jnp.where(line == place, 1.0, 0.0).astype(jnp.bfloat16)
    fold = lax.dot_general(
        jnp.ones((8, rows), jnp.bfloat16),
        selector[...],
        (((1,), (1,)), ((), ())),
        preferred_element_type=jnp.float32,
    )
    fold_core_out[...] = fold[:, 2 * BIN_DEV :]
    padded[:, 0:SPREAD] = jnp.zeros((2, SPREAD, 128), jnp.float32)
    padded[:, SPREAD + span :] = jnp.zeros((2, SPREAD, 128), jnp.float32)
    first_load.wait()
    weight_load(0).wait()
    load.start()
    lax.fori_loop(1, chunks, begin, 0)

    def core_copy(m):
        return pltpu.make_async_remote_copy(
            src_ref=send_core.at[m], dst_ref=recv_core.at[m],
            send_sem=core_send_sem.at[m], recv_sem=core_recv_sem.at[m],
            device_id={"cmp": core_peer}, device_id_type=MESH,
        )

    def x_copy(m):
        return pltpu.make_async_remote_copy(
            src_ref=send_x.at[m], dst_ref=recv_x.at[m],
            send_sem=x_send_sem.at[m], recv_sem=x_recv_sem.at[m],
            device_id={"cmp": x_peer}, device_id_type=MESH,
        )

    def z_copy(m):
        return pltpu.make_async_remote_copy(
            src_ref=send_z.at[m], dst_ref=recv_z.at[m],
            send_sem=z_send_sem.at[m], recv_sem=z_recv_sem.at[m],
            device_id={"off": lax.rem(z + nz - 1 - m // 2, nz)}, device_id_type=MESH,
        )

    def fold_copy(source, target, slot, device):
        return pltpu.make_async_remote_copy(
            src_ref=source, dst_ref=target,
            send_sem=fold_send_sem.at[slot], recv_sem=fold_recv_sem.at[slot],
            device_id=device, device_id_type=MESH,
        )

    def correct(m, source):
        first = pair_of(m) * WIDTH
        base = base_of(m)
        for half in range(2):
            start = starts_ref[2 * pair_of(m) + half]
            lead = jnp.clip(start - base, 0, SPREAD)
            padded[half, SPREAD : SPREAD + span] = weight[m, half].astype(jnp.float32)
            shifted_weight[:, half * 128 : half * 128 + 128] = padded[
                half, pl.ds(SPREAD - lead, band)
            ].astype(jnp.bfloat16)
        shifted = jnp.dot(source(), shifted_weight[...], preferred_element_type=jnp.float32)
        time = first + lax.broadcasted_iota(jnp.int32, (1, WIDTH), 1)
        taper = jnp.clip((time.astype(jnp.float32) - mute_ref[0]) / ramp_width, 0.0, 1.0)
        corrected = (shifted * taper).astype(jnp.bfloat16)
        partial = jnp.dot(selector[...], corrected, preferred_element_type=jnp.float32)
        keep_core[m] = partial[: 2 * BIN_DEV]
        send_core[m] = partial[2 * BIN_DEV :].astype(jnp.bfloat16)

    def end_core(m):
        core_copy(m).wait_recv()
        total = keep_core[m] + recv_core[m].astype(jnp.float32)
        keep_x[m] = total[:BIN_DEV]
        send_x[m] = total[BIN_DEV:].astype(jnp.bfloat16)
        x_copy(m).start()

    def x_total(m):
        x_copy(m).wait_recv()
        return keep_x[m] + recv_x[m].astype(jnp.float32)

    def end_x(m):
        send_z[m] = x_total(m).astype(jnp.bfloat16)
        z_copy(m).start()

    def later(m):
        weight_load(m).wait()
        correct(m, lambda: traces[:, pl.ds(pl.multiple_of(base_of(m), 128), band)])
        core_copy(m).start()
        end_core(m - 1)

    correct(0, lambda: first_band[...])
    pl.semaphore_wait(barrier, nz + 1)
    core_copy(0).start()
    fold_core = fold_copy(fold_core_out, fold_core_in, 0, {"cmp": core_peer})
    fold_core.start()
    load.wait()
    later(1)
    fold_core.wait_recv()
    fold = fold[:, : 2 * BIN_DEV] + fold_core_in[...]
    fold_x_out[0] = fold[:, BIN_DEV:]
    fold_x_out[1] = fold[:, :BIN_DEV]
    fold_x = fold_copy(fold_x_out.at[0], fold_x_in, 1, {"cmp": x_peer})
    fold_x.start()

    def step(m, carry):
        later(m)

        @pl.when(m >= 3)
        def _():
            end_x(m - 3)

        return carry

    lax.fori_loop(2, chunks, step, 0)
    end_core(chunks - 1)

    fold_x.wait_recv()
    fold = fold_x_out[1] + fold_x_in[...]
    fold_x_out[2] = fold
    fold_z = []
    for away in range(1, nz):
        copy = fold_copy(
            fold_x_out.at[2], fold_z_in.at[away - 1], 1 + away, {"off": lax.rem(z + away, nz)}
        )
        copy.start()
        fold_z.append(copy)
    for m in range(chunks - 3, chunks - 2):
        end_x(m)

    def drain(m, carry):
        core_copy(m).wait_send()
        return carry

    lax.fori_loop(0, chunks, drain, 0)
    fold_core.wait_send()
    fold_x.wait_send()
    for copy in fold_z:
        copy.wait_recv()
    for away in range(1, nz):
        fold = fold + fold_z_in[away - 1]
    fold_ref[...] = fold
    for copy in fold_z:
        copy.wait_send()

    def drain_x(m, carry):
        x_copy(m).wait_send()
        return carry

    lax.fori_loop(0, chunks - 2, drain_x, 0)
    early = [None, None]
    for m in range(chunks - 4):
        z_copy(m).wait_recv()
        z_copy(m).wait_send()
        arrived = recv_z[m].astype(jnp.float32)
        early[m % 2] = arrived if m < 2 else early[m % 2] + arrived
    for half in range(2):
        out_ref[:, half * WIDTH : half * WIDTH + WIDTH] = early[half]
    for m in range(chunks - 2, chunks):
        half = m % 2
        out_ref[:, half * WIDTH : half * WIDTH + WIDTH] += x_total(m)
    for m in range(chunks - 4, chunks - 2):
        half = m % 2
        z_copy(m).wait_recv()
        out_ref[:, half * WIDTH : half * WIDTH + WIDTH] += recv_z[m].astype(jnp.float32)
        z_copy(m).wait_send()
    for m in range(chunks - 2, chunks):
        x_copy(m).wait_send()


def on_device_fused(shot_traces, trace_owner, trace_bin, nmo_weight, band_start, mute_start):
    rows, samples = shot_traces.shape[1:]
    windows, span, ws = nmo_weight.shape[1:]
    chunks = samples // WIDTH
    f32, bf16 = jnp.float32, jnp.bfloat16
    hbm = pl.BlockSpec(memory_space=pltpu.HBM)
    vmem = pl.BlockSpec(memory_space=pltpu.VMEM)
    dma = pltpu.SemaphoreType.DMA
    totals, fold = pl.pallas_call(
        fused,
        out_shape=(
            jax.ShapeDtypeStruct((BIN_DEV, samples // 4), f32),
            jax.ShapeDtypeStruct((8, BIN_DEV), f32),
        ),
        in_specs=[hbm] * 6,
        out_specs=(vmem, vmem),
        scratch_shapes=[
            pltpu.VMEM((1, rows), jnp.int32),
            pltpu.VMEM((1, rows), jnp.int32),
            pltpu.SMEM((windows,), jnp.int32),
            pltpu.SMEM((1,), f32),
            pltpu.VMEM((rows, samples), bf16),
            pltpu.VMEM((rows, span + SPREAD), bf16),
            pltpu.VMEM((chunks, 2, span, ws), bf16),
            pltpu.VMEM((2, span + 2 * SPREAD, ws), f32),
            pltpu.VMEM((span + SPREAD, WIDTH), bf16),
            pltpu.VMEM((4 * BIN_DEV, rows), bf16),
            pltpu.VMEM((chunks, 2 * BIN_DEV, WIDTH), f32),
            pltpu.VMEM((chunks, 2 * BIN_DEV, WIDTH), bf16),
            pltpu.VMEM((chunks, 2 * BIN_DEV, WIDTH), bf16),
            pltpu.VMEM((chunks, BIN_DEV, WIDTH), f32),
            pltpu.VMEM((chunks, BIN_DEV, WIDTH), bf16),
            pltpu.VMEM((chunks, BIN_DEV, WIDTH), bf16),
            pltpu.VMEM((chunks - 2, BIN_DEV, WIDTH), bf16),
            pltpu.VMEM((chunks - 2, BIN_DEV, WIDTH), bf16),
            pltpu.VMEM((8, 2 * BIN_DEV), f32),
            pltpu.VMEM((8, 2 * BIN_DEV), f32),
            pltpu.VMEM((3, 8, BIN_DEV), f32),
            pltpu.VMEM((8, BIN_DEV), f32),
            pltpu.VMEM((3, 8, BIN_DEV), f32),
            dma,
            dma,
            dma((4,)),
            dma((chunks,)),
            dma((chunks,)),
            dma((chunks,)),
            dma((chunks,)),
            dma((chunks,)),
            dma((chunks - 2,)),
            dma((chunks - 2,)),
            dma((5,)),
            dma((5,)),
        ],
        compiler_params=pltpu.CompilerParams(
            collective_id=0, has_side_effects=True, vmem_limit_bytes=48 * 2**20
        ),
        cost_estimate=pl.CostEstimate(
            flops=4 * rows * samples * span, bytes_accessed=4 * rows * samples, transcendentals=0
        ),
    )(
        *(
            pltpu.with_memory_space_constraint(array, pltpu.HBM)
            for array in (
                shot_traces[0],
                nmo_weight[0],
                trace_owner.reshape(1, rows),
                trace_bin,
                band_start[0],
            )
        ),
        mute_start,
    )
    return totals / jnp.maximum(fold[0], 1.0)[:, None]


def solution(mesh):
    direct = mesh.shape["cmp"] == 4 and mesh.shape["off"] == 4
    return jax.shard_map(
        on_device_fused if direct else on_device,
        mesh=mesh,
        in_specs=(
            P(("groups", "off"), "cmp", None),
            P(("groups", "off"), "cmp", None),
            P(("groups", "off"), "cmp"),
            P("off", None, None, None),
            P("off", None),
            P("off"),
        ),
        out_specs=P(("groups", "cmp"), "off"),
        check_vma=False,
    )
```
